32 devices in a mesh: member: 2 (over y), patch: 4 (over z), rep: 2 (over x), sub: 2 (over core).
Axes of the slice: x: 2, y: 2, z: 4, core: 2. Of those that a mesh axis runs over, the one named last changes fastest.
Arguments:
- fine_latents: bfloat16 [16384, 512], P(('member', 'patch', 'rep', 'sub')), parts along dimension 0, may hold values from -6 to 6
- out_cotangent: bfloat16 [16384, 512], P(('member', 'patch', 'rep', 'sub')), parts along dimension 0, may hold values from -6 to 6
- weights: bfloat16 [3, 512, 512], replicated, may hold values from -0.25 to 0.25
- pool_index: int32 [8192], P(('patch', 'rep', 'sub')), may hold values from 0 to 511, as said below
- unpool_index: int32 [8192], P(('patch', 'rep', 'sub')), may hold values from 0 to 511, as said below
- senders: int32 [8192], P(('patch', 'rep', 'sub')), may hold values from 0 to 511, as said below
- receivers: int32 [8192], P(('patch', 'rep', 'sub')), may hold values from 0 to 511, as said below
- edge_valid: int32 [8192], P(('patch', 'rep', 'sub')), may hold values 0 or 1
Outputs:
- fine_grad: bfloat16 [16384, 512], P(('member', 'patch', 'rep', 'sub')), parts along dimension 0
- weight_grads: float32 [6, 512, 512], P('member', 'patch'), parts along dimension 0
The draws below stay inside these ranges and needn't reach their ends.
There are 2 independent parts, one for each index of `member`. The reference program is written for one: setup_inputs(seed, part) draws one part's arguments, and reference() takes and returns one part's arrays. A program takes and returns all parts, laid end to end along the dimension named above; an argument that names none is the same for every part. Nothing has to cross between parts.
Inputs may be any that keep to these rules, and one draw needn't show every extreme that they name: `pool_index`: fine node i pools into a coarse node of its own patch shard: between (i // 2048) * 128 and that plus 128 - 1. `unpool_index`: fine node i reads a coarse node of its own patch shard: between (i // 2048) * 128 and that plus 128 - 1. `senders`: with q = e // 2048 and shard q holding coarse nodes q * 128 to q * 128 + 127, the sender of slot e lies in shard q, or among the last 16 nodes of shard q - 1, or among the first 16 nodes of shard q + 1. `receivers`: the receiver of slot e lies in coarse shard e // 2048.
All inputs are finite; a program needn't handle non-finite values. No bound on the sum of `edge_valid` on one device may be relied on, other than what follows from the above.
Results may differ from the reference program's by a relative error of at most 0.014.
Values may be sent and summed in bfloat16 or wider, within the bound.
No kernel may reach another device: no remote copies, remote signals or barrier semaphores. Data moves between devices by JAX's collectives and lax.ppermute only.
A program may use at most 64 MiB of HBM per device.

```python
import jax
import jax.numpy as jnp
from jax import lax

D = 512
C_DEV = 128
RIM = 16
LAYERS = 2
NF = 8192
NC = 512
EDGES = 8192
FINE_SHARD = 2048
EDGE_SHARD = 2048
N_PATCH = 4


def draw_pool_index(key, part):
    key = jax.random.fold_in(key, 11)
    row_ids = jnp.arange(NF, dtype=jnp.int32)
    return row_ids // FINE_SHARD * C_DEV + jax.random.randint(key, (NF,), 0, C_DEV, dtype=jnp.int32)


def draw_unpool_index(key, part):
    key = jax.random.fold_in(key, 12)
    row_ids = jnp.arange(NF, dtype=jnp.int32)
    return row_ids // FINE_SHARD * C_DEV + jax.random.randint(key, (NF,), 0, C_DEV, dtype=jnp.int32)


def draw_senders(key, part):
    key = jax.random.fold_in(key, 13)
    key_kind, key_node, key_band = jax.random.split(key, 3)
    row_ids = jnp.arange(EDGES, dtype=jnp.int32)
    shard_ids = row_ids // EDGE_SHARD
    kinds = jax.random.randint(key_kind, (EDGES,), 0, 20, dtype=jnp.int32)
    own_node = shard_ids * C_DEV + jax.random.randint(key_node, (EDGES,), 0, C_DEV, dtype=jnp.int32)
    band_node = jax.random.randint(key_band, (EDGES,), 0, RIM, dtype=jnp.int32)
    from_prev = (shard_ids - 1) * C_DEV + C_DEV - RIM + band_node
    from_next = (shard_ids + 1) * C_DEV + band_node
    use_prev = (kinds == 0) & (shard_ids > 0)
    use_next = (kinds == 1) & (shard_ids < N_PATCH - 1)
    return jnp.where(use_prev, from_prev, jnp.where(use_next, from_next, own_node)).astype(jnp.int32)


def draw_receivers(key, part):
    key = jax.random.fold_in(key, 14)
    row_ids = jnp.arange(EDGES, dtype=jnp.int32)
    return row_ids // EDGE_SHARD * C_DEV + jax.random.randint(key, (EDGES,), 0, C_DEV, dtype=jnp.int32)


def set_ends(array, key, least, top_value):
    longest = array.shape.index(max(array.shape))
    spots = []
    for shift in (0, 1):
        where = [jax.random.randint(jax.random.fold_in(key, axis), (), 0, length) for axis, length in enumerate(array.shape)]
        where[longest] = (where[longest] + shift) % array.shape[longest]
        spots.append(tuple(where))
    return array.at[spots[0]].set(least).at[spots[1]].set(top_value)


def steps_of(rng, dims, cuts, least, largest):
    loudness, own = 1.0, jax.random.fold_in(rng, 6)
    for dim, blocks in cuts:
        steps = jnp.exp(jax.random.uniform(jax.random.fold_in(own, dim), (blocks,), jnp.float32, least / len(cuts), largest / len(cuts)))
        loudness = loudness * jnp.repeat(steps, dims[dim] // blocks).reshape([-1 if axis == dim else 1 for axis in range(len(dims))])
    return loudness


def centred(key, extent, scale, reach, cuts=(), held_as=jnp.bfloat16):
    entries = scale * jax.random.normal(key, extent, jnp.float32)
    if cuts:
        entries = entries * steps_of(key, extent, cuts, -0.22, 0.18)
    return jnp.clip(entries, -reach, reach).astype(held_as)


def setup_inputs(seed: int = 0, part: int = 0) -> dict:
    key_list = jax.random.split(jax.random.key(seed), 9)
    part_keys = jax.random.split(jax.random.fold_in(key_list[8], part), 9)
    return {
        "fine_latents": centred(part_keys[0], (NF, D), 1.0, 6.0, ((0, 16),)),
        "out_cotangent": centred(part_keys[1], (NF, D), 1.0, 6.0, ((0, 16),)),
        "weights": centred(key_list[2], (3, D, D), D ** -0.5, 0.25),
        "pool_index": draw_pool_index(jax.random.fold_in(key_list[8], 71), part),
        "unpool_index": draw_unpool_index(jax.random.fold_in(key_list[8], 71), part),
        "senders": draw_senders(jax.random.fold_in(key_list[8], 71), part),
        "receivers": draw_receivers(jax.random.fold_in(key_list[8], 71), part),
        "edge_valid": set_ends((jax.random.randint(key_list[7], (EDGES,), 0, 8) < 7).astype(jnp.int32), jax.random.fold_in(key_list[7], 1), 0, 1),
    }


def silu_slope(values):
    sigmoid_val = jax.nn.sigmoid(values)
    return sigmoid_val * (1.0 + values * (1.0 - sigmoid_val))


def exact_dot(left, right, contract):
    return lax.dot_general(left, right, (contract, ((), ())), precision=lax.Precision.HIGHEST, preferred_element_type=jnp.float32)


def reference(fine_latents, out_cotangent, weights, pool_index, unpool_index, senders, receivers, edge_valid):
    w_send = weights[0]
    w_recv = weights[1]
    w_unpool = weights[2]
    send_wide = w_send.astype(jnp.float32)
    recv_wide = w_recv.astype(jnp.float32)
    edge_mask = edge_valid.astype(jnp.float32)[:, None]
    coarse = 0.125 * jax.ops.segment_sum(fine_latents.astype(jnp.float32), pool_index, num_segments=NC)
    saved = []
    for layer_idx in range(LAYERS):
        rounded = coarse.astype(jnp.bfloat16)
        preact = jnp.dot(rounded[senders], w_send, preferred_element_type=jnp.float32) + jnp.dot(rounded[receivers], w_recv, preferred_element_type=jnp.float32)
        message = (edge_mask * jax.nn.silu(preact)).astype(jnp.bfloat16)
        incoming = jax.ops.segment_sum(message.astype(jnp.float32), receivers, num_segments=NC)
        saved.append((rounded, preact))
        coarse = coarse + 0.25 * incoming
    cotangent = out_cotangent.astype(jnp.float32)
    unpool_pre = jnp.dot(fine_latents, w_unpool, preferred_element_type=jnp.float32) + coarse[unpool_index]
    unpool_grad = (cotangent * silu_slope(unpool_pre)).astype(jnp.bfloat16)
    fine_grad = cotangent + lax.dot_general(unpool_grad, w_unpool, (((1,), (1,)), ((), ())), preferred_element_type=jnp.float32)
    grad_unpool = lax.dot_general(fine_latents, unpool_grad, (((0,), (0,)), ((), ())), preferred_element_type=jnp.float32)
    coarse_grad = jax.ops.segment_sum(unpool_grad.astype(jnp.float32), unpool_index, num_segments=NC)
    grad_send = jnp.zeros((D, D), jnp.float32)
    grad_recv = jnp.zeros((D, D), jnp.float32)
    for layer_idx in reversed(range(LAYERS)):
        rounded, preact = saved[layer_idx]
        msg_grad = edge_mask * 0.25 * coarse_grad[receivers]
        pre_grad = (msg_grad * silu_slope(preact)).astype(jnp.bfloat16)
        send_sums = jax.ops.segment_sum(pre_grad.astype(jnp.float32), senders, num_segments=NC)
        recv_sums = jax.ops.segment_sum(pre_grad.astype(jnp.float32), receivers, num_segments=NC)
        coarse_grad = coarse_grad + exact_dot(send_sums, send_wide, ((1,), (1,))) + exact_dot(recv_sums, recv_wide, ((1,), (1,)))
        rounded_wide = rounded.astype(jnp.float32)
        grad_send = grad_send + exact_dot(rounded_wide, send_sums, ((0,), (0,)))
        grad_recv = grad_recv + exact_dot(rounded_wide, recv_sums, ((0,), (0,)))
    fine_grad = fine_grad + 0.125 * coarse_grad[pool_index]
    return fine_grad.astype(jnp.bfloat16), jnp.stack([grad_send, grad_recv, grad_unpool])
```

```python
import jax
import jax.numpy as jnp
from jax import lax
from jax.sharding import PartitionSpec as P

D = 512
C_DEV = 128
RIM = 16
LAYERS = 2
BF16 = jnp.bfloat16
F32 = jnp.float32


def dot(left, right, contract=((1,), (0,))):
    return lax.dot_general(left, right, (contract, ((), ())), preferred_element_type=F32)


def split_pair(values):
    high = lax.optimization_barrier(values.astype(BF16))
    return high, (values - high.astype(F32)).astype(BF16)


def stacked_pair(values):
    return jnp.concatenate(split_pair(values), axis=0)


def hot_rows(indices, width):
    return (indices[:, None] == jnp.arange(width, dtype=jnp.int32)[None, :]).astype(BF16)


def hot_cols(indices, width):
    return (jnp.arange(width, dtype=jnp.int32)[:, None] == indices[None, :]).astype(BF16)


def exchange(x, axis, bit):
    return lax.ppermute(x, axis, [(i, i ^ bit) for i in range(lax.axis_size(axis))])


def bits_of(axis):
    return [1 << b for b in range(lax.axis_size(axis).bit_length() - 1)]


def group_sum(x):
    for bit in bits_of("sub"):
        x = x + exchange(x, "sub", bit)
    for bit in bits_of("rep"):
        x = x.astype(BF16)
        x = x.astype(F32) + exchange(x, "rep", bit).astype(F32)
    return x


def group_rows(x):
    for axis in ("sub", "rep"):
        for bit in bits_of(axis):
            other = exchange(x, axis, bit)
            first = (lax.axis_index(axis) & bit) == 0
            x = jnp.concatenate([jnp.where(first, x, other), jnp.where(first, other, x)], axis=-1)
    return x


def pair_trade(x, odd_pairs):
    patches, reps = lax.axis_size("patch"), lax.axis_size("rep")
    moves = []
    for q in range(patches):
        for r in range(reps):
            partner = (q ^ 1) if not odd_pairs else (((q + 1) ^ 1) - 1)
            if 0 <= partner < patches:
                moves.append((q * reps + r, partner * reps + r))
            else:
                moves.append((q * reps + r, q * reps + (r ^ 1)))
    return lax.ppermute(x, ("patch", "rep"), moves)


def trade_rims(to_prev, to_next):
    even = (lax.axis_index("patch") & 1) == 0
    first = pair_trade(jnp.where(even, to_next, to_prev), False)
    second = pair_trade(jnp.where(even, to_prev, to_next), True)
    return jnp.where(even, second, first), jnp.where(even, first, second)


def patch_scatter(x):
    patches = lax.axis_size("patch")
    if patches > 8:
        return lax.psum_scatter(x, "patch", scatter_dimension=1, tiled=True).astype(F32)
    kinds, rows, width = x.shape
    blocks = x.reshape(kinds, patches, rows // patches, width)
    here = lax.axis_index("patch")
    total = lax.dynamic_index_in_dim(blocks, here, 1, False).astype(F32)
    for step in range(1, patches):
        mine = lax.dynamic_index_in_dim(blocks, here ^ step, 1, False)
        total = total + exchange(mine, "patch", step).astype(F32)
    return total


def per_device(
    fine_latents, out_cotangent, weights, pool_index, unpool_index, senders, receivers, edge_valid
):
    w_send, w_recv, w_unpool = weights[0], weights[1], weights[2]
    reps, subs = lax.axis_size("rep"), lax.axis_size("sub")
    base = lax.axis_index("patch") * C_DEV
    pool_local = pool_index - base
    unpool_local = unpool_index - base
    valid = edge_valid != 0
    edges = jnp.stack([jnp.where(valid, receivers - base, -1), jnp.where(valid, senders - base, -C_DEV)])
    edges = group_rows(edges)
    recv, send = edges[0], edges[1]
    rim = jnp.where(send < 0, send + RIM, jnp.where(send >= C_DEV, send - C_DEV + RIM, -1))
    recv_rows, send_rows, rim_rows = hot_rows(recv, C_DEV), hot_rows(send, C_DEV), hot_rows(rim, 2 * RIM)
    gather_hot = jnp.concatenate([recv_rows, send_rows, recv_rows, send_rows, rim_rows, rim_rows], axis=1)
    back_hot = jnp.concatenate([recv_rows, recv_rows], axis=1)
    recv_cols = hot_cols(recv, C_DEV)
    sum_hot = jnp.concatenate([recv_cols, hot_cols(send, C_DEV), hot_cols(rim, 2 * RIM)], axis=0)

    coarse = 0.125 * group_sum(dot(hot_cols(pool_local, C_DEV), fine_latents))
    saved = []
    for layer in range(LAYERS):
        rounded = coarse.astype(BF16)
        before, after = trade_rims(rounded[:RIM], rounded[C_DEV - RIM :])
        rims = jnp.concatenate([before, after], axis=0)
        near_high, near_low = split_pair(0.5 * jnp.concatenate([dot(rounded, w_recv), dot(rounded, w_send)], axis=0))
        rim_high, rim_low = split_pair(0.5 * dot(rims, w_send))
        half = dot(gather_hot, jnp.concatenate([near_high, near_low, rim_high, rim_low], axis=0))
        tanh = jnp.tanh(half)
        message = (half + half * tanh).astype(BF16)
        slope = (0.5 * (1.0 + tanh) * (1.0 + half * (1.0 - tanh))).astype(BF16)
        saved.append((rounded, rims, slope))
        coarse = coarse + 0.25 * dot(recv_cols, message)

    cotangent = out_cotangent.astype(F32)
    unpool_rows = hot_rows(unpool_local, C_DEV)
    unpool_hot = jnp.concatenate([unpool_rows, unpool_rows], axis=1)
    unpool_half = 0.5 * (dot(fine_latents, w_unpool) + dot(unpool_hot, stacked_pair(coarse)))
    tanh = jnp.tanh(unpool_half)
    unpool_grad = (cotangent * (0.5 * (1.0 + tanh) * (1.0 + unpool_half * (1.0 - tanh)))).astype(BF16)
    coarse_grad = group_sum(dot(hot_cols(unpool_local, C_DEV), unpool_grad))
    fine_grad = cotangent + dot(unpool_grad, w_unpool, ((1,), (1,)))

    replica = lax.axis_index("rep") * subs + lax.axis_index("sub")
    width = D // (reps * subs)
    part = dot(fine_latents, unpool_grad, ((0,), (0,))).astype(BF16)
    for axis in ("rep", "sub"):
        for bit in reversed(bits_of(axis)):
            halves = part.reshape(D, 2, -1)
            upper = (lax.axis_index(axis) & bit) != 0
            kept = jnp.where(upper, halves[:, 1], halves[:, 0])
            given = jnp.where(upper, halves[:, 0], halves[:, 1])
            part = (kept.astype(F32) + exchange(given, axis, bit).astype(F32)).astype(BF16)

    send_left, send_right, recv_left, recv_right = [], [], [], []
    for layer in reversed(range(LAYERS)):
        rounded, rims, slope = saved[layer]
        pre_grad = (dot(back_hot, stacked_pair(0.25 * coarse_grad)) * slope.astype(F32)).astype(BF16)
        sums = dot(sum_hot, pre_grad)
        recv_sums, send_sums, rim_sums = sums[:C_DEV], sums[C_DEV : 2 * C_DEV], sums[2 * C_DEV :]
        block = lax.dynamic_slice_in_dim(sums, replica * width, width, 1)
        high, low = split_pair(block)
        window = jnp.concatenate([rounded, rims], axis=0)
        send_left += [window, window]
        send_right += [high[C_DEV:], low[C_DEV:]]
        recv_left += [rounded, rounded]
        recv_right += [high[:C_DEV], low[:C_DEV]]
        from_prev, from_next = trade_rims(rim_sums[:RIM].astype(BF16), rim_sums[RIM:].astype(BF16))
        gap = jnp.zeros((C_DEV - 2 * RIM, D), F32)
        send_sums = send_sums + jnp.concatenate([from_prev.astype(F32), gap, from_next.astype(F32)], axis=0)
        for total, matrix in ((send_sums, w_send), (recv_sums, w_recv)):
            high, low = split_pair(total)
            coarse_grad = coarse_grad + dot(high, matrix, ((1,), (1,))) + dot(low, matrix, ((1,), (1,)))
    first = ((0,), (0,))
    grads = jnp.stack(
        [
            dot(jnp.concatenate(send_left, axis=0), jnp.concatenate(send_right, axis=0), first).astype(BF16),
            dot(jnp.concatenate(recv_left, axis=0), jnp.concatenate(recv_right, axis=0), first).astype(BF16),
            part,
        ]
    )
    rows = patch_scatter(grads).astype(BF16)
    for axis in ("sub", "rep"):
        for bit in bits_of(axis):
            other = exchange(rows, axis, bit)
            lower = (lax.axis_index(axis) & bit) == 0
            rows = jnp.concatenate([jnp.where(lower, rows, other), jnp.where(lower, other, rows)], axis=2)
    pool_rows = hot_rows(pool_local, C_DEV)
    pool_hot = jnp.concatenate([pool_rows, pool_rows], axis=1)
    fine_grad = fine_grad + dot(pool_hot, stacked_pair(0.125 * coarse_grad))
    return fine_grad.astype(BF16), rows.astype(F32)


def solution(mesh):
    split = P(("patch", "rep", "sub"))
    rows = P(("member", "patch", "rep", "sub"), None)
    return jax.shard_map(
        per_device,
        mesh=mesh,
        in_specs=(rows, rows, P(), split, split, split, split, split),
        out_specs=(rows, P("member", "patch", None)),
        check_vma=False,
    )
```

```python
import functools

import jax
import jax.numpy as jnp
from jax import lax
from jax.experimental import pallas as pl
from jax.experimental.pallas import tpu as pltpu
from jax.sharding import PartitionSpec as P

D = 512
C_DEV = 128
RIM = 16
BF16 = jnp.bfloat16
F32 = jnp.float32
CHUNK = 512
ROWS = ((1,), (1,))
COLS = ((0,), (0,))
GATHER = 4 * C_DEV + 4 * RIM
SUMS = 2 * C_DEV + 2 * RIM


def dot(left, right, contract=((1,), (0,))):
    return lax.dot_general(left, right, (contract, ((), ())), preferred_element_type=F32)


def pair(values):
    high = values.astype(BF16)
    return high, (values - high.astype(F32)).astype(BF16)


def stacked(values):
    return jnp.concatenate(pair(values), axis=0)


def pair_dot(values, matrix, contract):
    high, low = pair(values)
    return dot(high, matrix, contract) + dot(low, matrix, contract)


def one_hot(mask):
    return jnp.where(mask, 1.0, 0.0).astype(BF16)


def iota(shape, dim):
    return lax.broadcasted_iota(jnp.int32, shape, dim)


def call(body, outs, *operands, scratch=(), limit=16):
    vmem = pl.BlockSpec(memory_space=pltpu.VMEM)
    return pl.pallas_call(
        body,
        out_shape=[jax.ShapeDtypeStruct(shape, dtype) for shape, dtype in outs],
        in_specs=[vmem] * len(operands),
        out_specs=[vmem] * len(outs),
        scratch_shapes=scratch,
        compiler_params=pltpu.CompilerParams(vmem_limit_bytes=limit << 20),
    )(*operands)


def node_base():
    return lax.axis_index("patch") * C_DEV


def even_patch():
    return (lax.axis_index("patch") & 1) == 0


def rim_place(send):
    return jnp.where(send < 0, send + RIM, jnp.where(send >= C_DEV, send - C_DEV + RIM, -1))


def columns_of(row):
    blocks = []
    for start in range(0, row.shape[1], 128):
        block = jnp.broadcast_to(row[:, start : start + 128].astype(F32), (128, 128))
        blocks.append(block.T)
    return jnp.concatenate(blocks, axis=0).astype(jnp.int32)


def store_rims(first_ref, second_ref, to_prev, to_next):
    even = even_patch()
    first_ref[...] = jnp.where(even, to_next, to_prev).astype(BF16)
    second_ref[...] = jnp.where(even, to_prev, to_next).astype(BF16)


def load_rims(first_ref, second_ref):
    even = even_patch()
    first, second = first_ref[...].astype(F32), second_ref[...].astype(F32)
    return jnp.where(even, second, first), jnp.where(even, first, second)


def pool_kernel(fine_ref, pool_ref, send_ref, recv_ref, valid_ref, pooled_ref, edges_ref):
    base = node_base()
    rows = fine_ref.shape[0]
    hot = one_hot(iota((C_DEV, rows), 0) == pool_ref[...] - base)
    pooled_ref[...] = dot(hot, fine_ref[...])
    valid = valid_ref[...] != 0
    edges_ref[0:1, :] = jnp.where(valid, recv_ref[...] - base, -1)
    edges_ref[1:2, :] = jnp.where(valid, send_ref[...] - base, -C_DEV)


def hots_kernel(edges_ref, gather_ref, sum_ref):
    for start in range(0, edges_ref.shape[1], CHUNK):
        part = pl.ds(start, CHUNK)
        recv, send = edges_ref[0:1, part], edges_ref[1:2, part]
        node = iota((C_DEV, CHUNK), 0)
        sum_ref[0:C_DEV, part] = one_hot(node == recv)
        sum_ref[C_DEV : 2 * C_DEV, part] = one_hot(node == send)
        sum_ref[2 * C_DEV :, part] = one_hot(iota((2 * RIM, CHUNK), 0) == rim_place(send))
        recv, send = columns_of(recv), columns_of(send)
        node = iota((CHUNK, C_DEV), 1)
        receiver, sender = one_hot(node == recv), one_hot(node == send)
        gather_ref[part, 0:C_DEV] = sender
        gather_ref[part, C_DEV : 2 * C_DEV] = receiver
        gather_ref[part, 2 * C_DEV : 3 * C_DEV] = receiver
        gather_ref[part, 3 * C_DEV : 4 * C_DEV] = sender
        place = iota((CHUNK, 4 * RIM), 1) & (2 * RIM - 1)
        gather_ref[part, 4 * C_DEV :] = one_hot(place == rim_place(send[:, : 4 * RIM]))


def start_kernel(own_ref, other_ref, coarse_ref, first_ref, second_ref):
    coarse = 0.125 * (own_ref[...].astype(F32) + other_ref[...].astype(F32))
    coarse_ref[...] = coarse
    store_rims(first_ref, second_ref, coarse[:RIM], coarse[C_DEV - RIM :])


def layer_forward(gather_ref, sum_ref, coarse_ref, got_first_ref, got_second_ref, w_ref, slope_ref, message_ref):
    coarse = coarse_ref[...]
    rounded = coarse.astype(BF16)
    rims = jnp.concatenate(load_rims(got_first_ref, got_second_ref), axis=0).astype(BF16)
    send_high, send_low = pair(0.5 * dot(rounded, w_ref[0]))
    recv_high, recv_low = pair(0.5 * dot(rounded, w_ref[1]))
    rim_high, rim_low = pair(0.5 * dot(rims, w_ref[0]))
    table = jnp.concatenate([send_high, recv_high, recv_low, send_low, rim_high, rim_low], axis=0)
    for start in range(0, gather_ref.shape[0], CHUNK):
        part = pl.ds(start, CHUNK)
        half = dot(gather_ref[part, :], table)
        tanh = jnp.tanh(half)
        message_ref[part, :] = (half + half * tanh).astype(BF16)
        slope_ref[part, :] = ((0.5 + 0.5 * tanh) * (1.0 + half * (1.0 - tanh))).astype(BF16)
    return coarse + 0.25 * dot(sum_ref[0:C_DEV, :], message_ref[...])


def first_forward_kernel(
    gather_ref, sum_ref, coarse_ref, got_first_ref, got_second_ref, w_ref,
    new_ref, slope_ref, first_ref, second_ref, message_ref,
):
    coarse = layer_forward(
        gather_ref, sum_ref, coarse_ref, got_first_ref, got_second_ref, w_ref, slope_ref, message_ref
    )
    new_ref[...] = coarse
    store_rims(first_ref, second_ref, coarse[:RIM], coarse[C_DEV - RIM :])


def last_forward_kernel(
    gather_ref, sum_ref, coarse_ref, got_first_ref, got_second_ref, w_ref, fine_ref, cotangent_ref, unpool_ref,
    slope_ref, unpool_grad_ref, partial_ref, message_ref,
):
    coarse = layer_forward(
        gather_ref, sum_ref, coarse_ref, got_first_ref, got_second_ref, w_ref, slope_ref, message_ref
    )
    rows = fine_ref.shape[0]
    unpool = unpool_ref[...] - node_base()
    hot = one_hot(iota((rows, C_DEV), 1) == columns_of(unpool))
    half = 0.5 * (dot(fine_ref[...], w_ref[2]) + dot(jnp.concatenate([hot, hot], axis=1), stacked(coarse)))
    tanh = jnp.tanh(half)
    slope = (0.5 + 0.5 * tanh) * (1.0 + half * (1.0 - tanh))
    grad = (cotangent_ref[...].astype(F32) * slope).astype(BF16)
    unpool_grad_ref[...] = grad
    partial_ref[...] = dot(one_hot(iota((C_DEV, rows), 0) == unpool), grad)


def halves(values, bit):
    middle = values.shape[1] // 2
    lower, upper = values[:, :middle], values[:, middle:]
    return jnp.where(bit, upper, lower), jnp.where(bit, lower, upper)


def unpool_kernel(fine_ref, cotangent_ref, unpool_grad_ref, w_ref, base_ref, kept_ref, given_ref):
    grad = unpool_grad_ref[...]
    base_ref[...] = cotangent_ref[...].astype(F32) + dot(grad, w_ref[2], ROWS)
    kept, given = halves(dot(fine_ref[...], grad, COLS), lax.axis_index("sub") != 0)
    kept_ref[...] = kept.astype(BF16)
    given_ref[...] = given.astype(BF16)


def halve_kernel(bit, own_ref, other_ref, kept_ref, given_ref):
    total = own_ref[...].astype(F32) + other_ref[...].astype(F32)
    kept, given = halves(total, (lax.axis_index("rep") & bit) != 0)
    kept_ref[...] = kept.astype(BF16)
    given_ref[...] = given.astype(BF16)


def replica_index():
    return lax.axis_index("sub") * lax.axis_size("rep") + lax.axis_index("rep")


def column_block(sums_ref, width):
    if width % 128 == 0:
        return sums_ref[:, pl.ds(pl.multiple_of(replica_index() * width, 128), width)]
    block = sums_ref[:, :width]
    for at in range(1, D // width):
        block = jnp.where(replica_index() == at, sums_ref[:, at * width : (at + 1) * width], block)
    return block


def layer_backward(gather_ref, sum_ref, slope_ref, grad, pre_ref, sums_ref):
    table = stacked(0.25 * grad)
    for start in range(0, gather_ref.shape[0], CHUNK):
        part = pl.ds(start, CHUNK)
        flowing = dot(gather_ref[part, C_DEV : 3 * C_DEV], table)
        pre_ref[part, :] = (flowing * slope_ref[part, :].astype(F32)).astype(BF16)
    sums_ref[...] = dot(sum_ref[...], pre_ref[...])


def weight_blocks(sums_ref, coarse_ref, got_first_ref, got_second_ref, width):
    rounded = coarse_ref[...].astype(BF16)
    rims = jnp.concatenate(load_rims(got_first_ref, got_second_ref), axis=0).astype(BF16)
    block = column_block(sums_ref, width)
    double = jnp.concatenate([rounded, rounded], axis=0)
    recv = dot(double, stacked(block[:C_DEV]), COLS)
    send = dot(double, stacked(block[C_DEV : 2 * C_DEV]), COLS)
    send = send + dot(jnp.concatenate([rims, rims], axis=0), stacked(block[2 * C_DEV :]), COLS)
    return send, recv


def last_backward_kernel(
    gather_ref, sum_ref, slope_ref, own_ref, other_ref, coarse_ref, got_first_ref, got_second_ref,
    grad_ref, sums_ref, blocks_ref, first_ref, second_ref, pre_ref,
):
    grad = own_ref[...].astype(F32) + other_ref[...].astype(F32)
    grad_ref[...] = grad
    layer_backward(gather_ref, sum_ref, slope_ref, grad, pre_ref, sums_ref)
    store_rims(first_ref, second_ref, sums_ref[2 * C_DEV : 2 * C_DEV + RIM, :], sums_ref[2 * C_DEV + RIM :, :])
    send, recv = weight_blocks(sums_ref, coarse_ref, got_first_ref, got_second_ref, blocks_ref.shape[2])
    blocks_ref[0] = send
    blocks_ref[1] = recv


def project(grad, sums_ref, got_first_ref, got_second_ref, w_ref):
    from_prev, from_next = load_rims(got_first_ref, got_second_ref)
    gap = jnp.zeros((C_DEV - 2 * RIM, D), F32)
    send = sums_ref[C_DEV : 2 * C_DEV, :] + jnp.concatenate([from_prev, gap, from_next], axis=0)
    return grad + pair_dot(send, w_ref[0], ROWS) + pair_dot(sums_ref[0:C_DEV, :], w_ref[1], ROWS)


def first_backward_kernel(
    gather_ref, sum_ref, slope_ref, upper_grad_ref, upper_sums_ref, got_first_ref, got_second_ref, w_ref,
    coarse_ref, rim_first_ref, rim_second_ref, upper_blocks_ref, kept_ref, given_ref,
    grad_ref, sums_ref, first_ref, second_ref, *refs,
):
    *out_refs, pre_ref, blocks_ref = refs
    grad = project(upper_grad_ref[...], upper_sums_ref, got_first_ref, got_second_ref, w_ref)
    grad_ref[...] = grad
    layer_backward(gather_ref, sum_ref, slope_ref, grad, pre_ref, sums_ref)
    store_rims(first_ref, second_ref, sums_ref[2 * C_DEV : 2 * C_DEV + RIM, :], sums_ref[2 * C_DEV + RIM :, :])
    send, recv = weight_blocks(sums_ref, coarse_ref, rim_first_ref, rim_second_ref, blocks_ref.shape[2])
    blocks_ref[0] = upper_blocks_ref[0] + send
    blocks_ref[1] = upper_blocks_ref[1] + recv
    blocks_ref[2] = kept_ref[...].astype(F32) + given_ref[...].astype(F32)
    if len(out_refs) == 1:
        out_refs[0][...] = blocks_ref[...].astype(BF16)
        return
    rows = D // len(out_refs)
    for step, ref in enumerate(out_refs):
        start = pl.multiple_of((lax.axis_index("patch") ^ step) * rows, rows)
        ref[...] = blocks_ref[:, pl.ds(start, rows), :].astype(BF16)


def finish_kernel(grad_ref, sums_ref, got_first_ref, got_second_ref, w_ref, pool_ref, base_ref, out_ref):
    grad = project(grad_ref[...], sums_ref, got_first_ref, got_second_ref, w_ref)
    rows = base_ref.shape[0]
    hot = one_hot(iota((rows, C_DEV), 1) == columns_of(pool_ref[...] - node_base()))
    pulled = dot(jnp.concatenate([hot, hot], axis=1), stacked(0.125 * grad))
    out_ref[...] = (base_ref[...] + pulled).astype(BF16)


def exchange(x, axis, bit):
    return lax.ppermute(x, axis, [(i, i ^ bit) for i in range(lax.axis_size(axis))])


def bits_of(axis):
    return [1 << b for b in range(lax.axis_size(axis).bit_length() - 1)]


def group_sum(x):
    for bit in bits_of("sub"):
        x = x + exchange(x, "sub", bit)
    x = x.astype(BF16)
    *early, last = bits_of("rep")
    for bit in early:
        x = (x.astype(F32) + exchange(x, "rep", bit).astype(F32)).astype(BF16)
    return x, exchange(x, "rep", last)


def group_edges(x):
    for axis in ("sub", "rep"):
        for bit in bits_of(axis):
            x = jnp.concatenate([x, exchange(x, axis, bit)], axis=1)
    return x


def pair_trade(x, odd_pairs):
    patches, reps = lax.axis_size("patch"), lax.axis_size("rep")
    moves = []
    for q in range(patches):
        for r in range(reps):
            partner = (q ^ 1) if not odd_pairs else (((q + 1) ^ 1) - 1)
            if 0 <= partner < patches:
                moves.append((q * reps + r, partner * reps + r))
            else:
                moves.append((q * reps + r, q * reps + (r ^ 1)))
    return lax.ppermute(x, ("patch", "rep"), moves)


def trade(first, second):
    return pair_trade(first, False), pair_trade(second, True)


def place_kernel(*refs):
    *blocks, out_ref = refs
    width = blocks[0].shape[2]
    for mask, ref in enumerate(blocks):
        start = pl.multiple_of((replica_index() ^ mask) * width, width)
        out_ref[:, :, pl.ds(start, width)] = ref[...].astype(F32)


def group_columns(x):
    blocks = [x]
    for axis in ("rep", "sub"):
        for bit in bits_of(axis):
            blocks = blocks + [exchange(block, axis, bit) for block in blocks]
    kinds, rows, width = x.shape
    if width % 128 == 0:
        return call(place_kernel, [((kinds, rows, D), F32)], *blocks)[0]
    order = jnp.arange(len(blocks)) ^ replica_index()
    ordered = jnp.take(jnp.stack(blocks), order, axis=0)
    return jnp.moveaxis(ordered, 0, 2).reshape(kinds, rows, D).astype(F32)


def per_device(
    fine_latents, out_cotangent, weights, pool_index, unpool_index, senders, receivers, edge_valid
):
    patches, reps, subs = (lax.axis_size(axis) for axis in ("patch", "rep", "sub"))
    rows = fine_latents.shape[0]
    slots = senders.shape[0]
    edges = slots * reps * subs
    width = D // (reps * subs)
    pool_row, unpool_row = pool_index[None, :], unpool_index[None, :]
    rim = ((RIM, D), BF16)
    coarse_out = ((C_DEV, D), F32)
    sums_out = ((SUMS, D), F32)
    work = [pltpu.VMEM((edges, D), BF16)]

    pooled, own_edges = call(
        pool_kernel, [coarse_out, ((2, slots), jnp.int32)],
        fine_latents, pool_row, senders[None, :], receivers[None, :], edge_valid[None, :],
    )
    own, other = group_sum(pooled)
    gather_hot, sum_hot = call(
        hots_kernel, [((edges, GATHER), BF16), ((SUMS, edges), BF16)], group_edges(own_edges)
    )
    other, gather_hot, sum_hot = lax.optimization_barrier((other, gather_hot, sum_hot))
    coarse_0, first, second = call(start_kernel, [coarse_out, rim, rim], own, other)
    rims_0 = trade(first, second)
    coarse_1, slope_1, first, second = call(
        first_forward_kernel, [coarse_out, ((edges, D), BF16), rim, rim],
        gather_hot, sum_hot, coarse_0, *rims_0, weights, scratch=work,
    )
    rims_1 = trade(first, second)
    slope_2, unpool_grad, partial = call(
        last_forward_kernel, [((edges, D), BF16), ((rows, D), BF16), coarse_out],
        gather_hot, sum_hot, coarse_1, *rims_1, weights, fine_latents, out_cotangent, unpool_row, scratch=work,
    )
    own, other = group_sum(partial)
    fine_base, kept, given = call(
        unpool_kernel, [((rows, D), F32), ((D, D // 2), BF16), ((D, D // 2), BF16)],
        fine_latents, out_cotangent, unpool_grad, weights,
    )
    other, given = lax.optimization_barrier((other, given))
    given = exchange(given, "sub", 1)
    grad_2, sums_2, blocks_2, first, second = call(
        last_backward_kernel, [coarse_out, sums_out, ((2, D, width), F32), rim, rim],
        gather_hot, sum_hot, slope_2, own, other, coarse_1, *rims_1, scratch=work,
    )
    for bit in reversed(bits_of("rep")):
        half = ((D, kept.shape[1] // 2), BF16)
        kept, given = call(functools.partial(halve_kernel, bit), [half, half], kept, given)
        given, first, second = lax.optimization_barrier((given, first, second))
        given = exchange(given, "rep", bit)
    got = trade(first, second)
    blocks = patches if patches <= 8 else 1
    outs = call(
        first_backward_kernel,
        [coarse_out, sums_out, rim, rim] + [((3, D // blocks, width), BF16)] * blocks,
        gather_hot, sum_hot, slope_1, grad_2, sums_2, *got, weights, coarse_0, *rims_0, blocks_2, kept, given,
        scratch=work + [pltpu.VMEM((3, D, width), F32)],
    )
    grad_1, sums_1, first, second, *blocks = outs
    if len(blocks) == 1:
        total = lax.psum_scatter(blocks[0], "patch", scatter_dimension=1, tiled=True)
    else:
        total = blocks[0].astype(F32)
        for step, block in enumerate(blocks):
            if step:
                total = total + exchange(block, "patch", step).astype(F32)
        total = total.astype(BF16)
    got = trade(first, second)
    weight_grads = group_columns(total)
    fine_grad = call(
        finish_kernel, [((rows, D), BF16)], grad_1, sums_1, *got, weights, pool_row, fine_base
    )[0]
    return fine_grad, weight_grads


def solution(mesh):
    split = P(("patch", "rep", "sub"))
    rows = P(("member", "patch", "rep", "sub"), None)
    return jax.shard_map(
        per_device,
        mesh=mesh,
        in_specs=(rows, rows, P(), split, split, split, split, split),
        out_specs=(rows, P("member", "patch", None)),
        check_vma=False,
    )
```

```python
import functools

import jax
import jax.numpy as jnp
from jax import lax
from jax.experimental import pallas as pl
from jax.experimental.pallas import tpu as pltpu
from jax.sharding import PartitionSpec as P

D = 512
C_DEV = 128
RIM = 16
BF16 = jnp.bfloat16
F32 = jnp.float32
CHUNK = 512
ROWS = ((1,), (1,))
COLS = ((0,), (0,))
GATHER = 4 * C_DEV + 4 * RIM
SUMS = 2 * C_DEV + 2 * RIM


def dot(left, right, contract=((1,), (0,))):
    return lax.dot_general(left, right, (contract, ((), ())), preferred_element_type=F32)


def pair(values):
    high = values.astype(BF16)
    return high, (values - high.astype(F32)).astype(BF16)


def stacked(values):
    return jnp.concatenate(pair(values), axis=0)


def pair_dot(values, matrix, contract):
    high, low = pair(values)
    return dot(high, matrix, contract) + dot(low, matrix, contract)


def one_hot(mask):
    return jnp.where(mask, 1.0, 0.0).astype(BF16)


def iota(shape, dim):
    return lax.broadcasted_iota(jnp.int32, shape, dim)


def call(body, outs, *operands, scratch=(), limit=16):
    vmem = pl.BlockSpec(memory_space=pltpu.VMEM)
    return pl.pallas_call(
        body,
        out_shape=[jax.ShapeDtypeStruct(shape, dtype) for shape, dtype in outs],
        in_specs=[pl.BlockSpec(memory_space=pltpu.VMEM)] * len(operands),
        out_specs=[vmem] * len(outs),
        scratch_shapes=scratch,
        compiler_params=pltpu.CompilerParams(vmem_limit_bytes=limit << 20),
    )(*operands)


def node_base():
    return lax.axis_index("patch") * C_DEV


def even_patch():
    return (lax.axis_index("patch") & 1) == 0


def rim_place(send):
    return jnp.where(send < 0, send + RIM, jnp.where(send >= C_DEV, send - C_DEV + RIM, -1))


def columns_of(row):
    blocks = []
    for start in range(0, row.shape[1], 128):
        block = jnp.broadcast_to(row[:, start : start + 128].astype(F32), (128, 128))
        blocks.append(block.T)
    return jnp.concatenate(blocks, axis=0).astype(jnp.int32)


def store_rims(first_ref, second_ref, to_prev, to_next):
    even = even_patch()
    first_ref[...] = jnp.where(even, to_next, to_prev).astype(BF16)
    second_ref[...] = jnp.where(even, to_prev, to_next).astype(BF16)


def load_rims(first_ref, second_ref):
    even = even_patch()
    first, second = first_ref[...].astype(F32), second_ref[...].astype(F32)
    return jnp.where(even, second, first), jnp.where(even, first, second)


def edges_kernel(send_ref, recv_ref, valid_ref, edges_ref):
    base = node_base()
    valid = valid_ref[...] != 0
    edges_ref[0:1, :] = jnp.where(valid, recv_ref[...] - base, -1)
    edges_ref[1:2, :] = jnp.where(valid, send_ref[...] - base, -C_DEV)


def hots_kernel(edges_ref, w_ref, gather_ref, sum_ref):
    del w_ref
    for start in range(0, edges_ref.shape[1], CHUNK):
        part = pl.ds(start, CHUNK)
        recv, send = edges_ref[0:1, part], edges_ref[1:2, part]
        node = iota((C_DEV, CHUNK), 0)
        sum_ref[0:C_DEV, part] = one_hot(node == recv)
        sum_ref[C_DEV : 2 * C_DEV, part] = one_hot(node == send)
        sum_ref[2 * C_DEV :, part] = one_hot(iota((2 * RIM, CHUNK), 0) == rim_place(send))
        recv, send = columns_of(recv), columns_of(send)
        node = iota((CHUNK, C_DEV), 1)
        receiver, sender = one_hot(node == recv), one_hot(node == send)
        gather_ref[part, 0:C_DEV] = sender
        gather_ref[part, C_DEV : 2 * C_DEV] = receiver
        gather_ref[part, 2 * C_DEV : 3 * C_DEV] = receiver
        gather_ref[part, 3 * C_DEV : 4 * C_DEV] = sender
        place = iota((CHUNK, 4 * RIM), 1) & (2 * RIM - 1)
        gather_ref[part, 4 * C_DEV :] = one_hot(place == rim_place(send[:, : 4 * RIM]))


def pooled_kernel(own_ref, other_ref, part_ref, first_ref, second_ref):
    part = 0.125 * (own_ref[...] + other_ref[...])
    part_ref[...] = part.astype(BF16)
    store_rims(first_ref, second_ref, part[:RIM], part[C_DEV - RIM :])


def total(refs):
    return sum(ref[...].astype(F32) for ref in refs)


def near_tables(coarse, w_ref):
    rounded = coarse.astype(BF16)
    send_high, send_low = pair(0.5 * dot(rounded, w_ref[0]))
    recv_high, recv_low = pair(0.5 * dot(rounded, w_ref[1]))
    return jnp.concatenate([send_high, recv_high, recv_low, send_low], axis=0)


def first_near_kernel(gather_ref, w_ref, *refs):
    *part_refs, coarse_ref, near_ref = refs
    coarse = total(part_refs)
    coarse_ref[...] = coarse
    near_ref[...] = dot(gather_ref[:, 0 : 4 * C_DEV], near_tables(coarse, w_ref))


def near_kernel(
    gather_ref, w_ref, coarse_ref, fine_ref, unpool_ref, near_ref, fine_half_ref, hot_rows_ref, hot_cols_ref
):
    near_ref[...] = dot(gather_ref[:, 0 : 4 * C_DEV], near_tables(coarse_ref[...], w_ref))
    fine_half_ref[...] = 0.5 * dot(fine_ref[...], w_ref[2])
    rows = fine_ref.shape[0]
    unpool = unpool_ref[...] - node_base()
    hot = one_hot(iota((rows, C_DEV), 1) == columns_of(unpool))
    hot_rows_ref[:, 0:C_DEV] = hot
    hot_rows_ref[:, C_DEV:] = hot
    hot_cols_ref[...] = one_hot(iota((C_DEV, rows), 0) == unpool)


def layer_forward(gather_ref, sum_ref, near_ref, coarse_ref, rims, w_ref, slope_ref, rims_ref, message_ref):
    rims = rims.astype(BF16)
    rims_ref[...] = rims
    table = stacked(0.5 * dot(rims, w_ref[0]))
    for start in range(0, gather_ref.shape[0], CHUNK):
        part = pl.ds(start, CHUNK)
        half = near_ref[part, :] + dot(gather_ref[part, 4 * C_DEV :], table)
        tanh = jnp.tanh(half)
        message_ref[part, :] = (half + half * tanh).astype(BF16)
        slope_ref[part, :] = ((0.5 + 0.5 * tanh) * (1.0 + half * (1.0 - tanh))).astype(BF16)
    return coarse_ref[...] + 0.25 * dot(sum_ref[0:C_DEV, :], message_ref[...])


def first_forward_kernel(gather_ref, sum_ref, near_ref, coarse_ref, w_ref, *refs):
    *got_refs, new_ref, slope_ref, rims_ref, first_ref, second_ref, message_ref = refs
    rims = jnp.concatenate(
        [sum(parts) for parts in zip(*(load_rims(*got) for got in zip(got_refs[::2], got_refs[1::2])))], axis=0
    )
    coarse = layer_forward(gather_ref, sum_ref, near_ref, coarse_ref, rims, w_ref, slope_ref, rims_ref, message_ref)
    new_ref[...] = coarse
    store_rims(first_ref, second_ref, coarse[:RIM], coarse[C_DEV - RIM :])


def last_forward_kernel(
    gather_ref, sum_ref, near_ref, coarse_ref, w_ref, got_first_ref, got_second_ref,
    fine_half_ref, hot_rows_ref, hot_cols_ref, cotangent_ref,
    slope_ref, rims_ref, unpool_grad_ref, partial_ref, message_ref,
):
    rims = jnp.concatenate(load_rims(got_first_ref, got_second_ref), axis=0)
    coarse = layer_forward(gather_ref, sum_ref, near_ref, coarse_ref, rims, w_ref, slope_ref, rims_ref, message_ref)
    half = fine_half_ref[...] + dot(hot_rows_ref[...], stacked(0.5 * coarse))
    tanh = jnp.tanh(half)
    slope = (0.5 + 0.5 * tanh) * (1.0 + half * (1.0 - tanh))
    grad = (cotangent_ref[...].astype(F32) * slope).astype(BF16)
    unpool_grad_ref[...] = grad
    partial_ref[...] = dot(hot_cols_ref[...], grad)


def halves(values, bit):
    middle = values.shape[1] // 2
    lower, upper = values[:, :middle], values[:, middle:]
    return jnp.where(bit, upper, lower), jnp.where(bit, lower, upper)


def unpool_kernel(fine_ref, cotangent_ref, unpool_grad_ref, w_ref, base_ref, kept_ref, given_ref):
    grad = unpool_grad_ref[...]
    base_ref[...] = cotangent_ref[...].astype(F32) + dot(grad, w_ref[2], ROWS)
    kept, given = halves(dot(fine_ref[...], grad, COLS), lax.axis_index("sub") != 0)
    kept_ref[...] = kept.astype(BF16)
    given_ref[...] = given.astype(BF16)


def halve_kernel(bit, own_ref, other_ref, kept_ref, given_ref):
    total = own_ref[...].astype(F32) + other_ref[...].astype(F32)
    kept, given = halves(total, (lax.axis_index("rep") & bit) != 0)
    kept_ref[...] = kept.astype(BF16)
    given_ref[...] = given.astype(BF16)


def replica_index():
    return lax.axis_index("sub") * lax.axis_size("rep") + lax.axis_index("rep")


def column_block(ref, width):
    if width % 128 == 0:
        return ref[:, pl.ds(pl.multiple_of(replica_index() * width, 128), width)]
    block = ref[:, :width]
    for at in range(1, D // width):
        block = jnp.where(replica_index() == at, ref[:, at * width : (at + 1) * width], block)
    return block


def layer_backward(gather_ref, sum_ref, slope_ref, grad, pre_ref, sums_ref):
    table = stacked(0.25 * grad)
    for start in range(0, gather_ref.shape[0], CHUNK):
        part = pl.ds(start, CHUNK)
        flowing = dot(gather_ref[part, C_DEV : 3 * C_DEV], table)
        pre_ref[part, :] = (flowing * slope_ref[part, :].astype(F32)).astype(BF16)
    sums_ref[...] = dot(sum_ref[...], pre_ref[...])


def turned_window(coarse_ref, rims_ref):
    rounded, rims = coarse_ref[...].astype(BF16).astype(F32), rims_ref[...].astype(F32)
    own, rims = rounded.T.astype(BF16), rims.T.astype(BF16)
    return jnp.concatenate([own, own, rims, rims], axis=1)


def weight_blocks(block, turned):
    recv = dot(turned[:, : 2 * C_DEV], stacked(block[:C_DEV]))
    send = jnp.concatenate([stacked(block[C_DEV : 2 * C_DEV]), stacked(block[2 * C_DEV :])], axis=0)
    return dot(turned, send), recv


def store_rim_sums(first_ref, second_ref, sums_ref):
    store_rims(first_ref, second_ref, sums_ref[2 * C_DEV : 2 * C_DEV + RIM, :], sums_ref[2 * C_DEV + RIM :, :])


def last_backward_kernel(
    gather_ref, sum_ref, slope_ref, own_ref, other_ref, grad_ref, sums_ref, first_ref, second_ref, pre_ref
):
    grad = own_ref[...].astype(F32) + other_ref[...].astype(F32)
    grad_ref[...] = grad
    layer_backward(gather_ref, sum_ref, slope_ref, grad, pre_ref, sums_ref)
    store_rim_sums(first_ref, second_ref, sums_ref)


def project(grad, send, recv, send_matrix, recv_matrix):
    return grad + pair_dot(send, send_matrix, ROWS) + pair_dot(recv, recv_matrix, ROWS)


def matrix_block(w_ref, kind, width):
    return w_ref[kind, pl.ds(pl.multiple_of(replica_index() * width, width), width), :]


def middle_kernel(
    gather_ref, grad_ref, sums_ref, w_ref, upper_coarse_ref, upper_rims_ref, coarse_ref, rims_ref,
    blocks_ref, turned_ref, flowing_ref,
):
    width = blocks_ref.shape[2]
    turned_ref[...] = turned_window(coarse_ref, rims_ref)
    send, recv = weight_blocks(column_block(sums_ref, width), turned_window(upper_coarse_ref, upper_rims_ref))
    blocks_ref[0] = send
    blocks_ref[1] = recv
    grad = project(
        column_block(grad_ref, width), sums_ref[C_DEV : 2 * C_DEV, :], sums_ref[0:C_DEV, :],
        matrix_block(w_ref, 0, width), matrix_block(w_ref, 1, width),
    )
    flowing_ref[...] = dot(gather_ref[:, C_DEV : 3 * C_DEV], stacked(0.25 * grad))


def rim_totals(got_first_ref, got_second_ref):
    from_prev, from_next = load_rims(got_first_ref, got_second_ref)
    return jnp.concatenate([from_prev, jnp.zeros((C_DEV - 2 * RIM, D), F32), from_next], axis=0)


def block_backward_kernel(
    gather_ref, sum_ref, slope_ref, flowing_ref, got_first_ref, got_second_ref, w_ref, turned_ref, upper_blocks_ref,
    kept_ref, given_ref, *refs,
):
    *out_refs, blocks_ref = refs
    width = blocks_ref.shape[2]
    rims = rim_totals(got_first_ref, got_second_ref).astype(BF16)
    incoming = dot(rims, matrix_block(w_ref, 0, width), ROWS)
    flowing = flowing_ref[...] + dot(gather_ref[:, C_DEV : 3 * C_DEV], stacked(0.25 * incoming))
    pre_grad = (flowing * column_block(slope_ref, width).astype(F32)).astype(BF16)
    send, recv = weight_blocks(dot(sum_ref[...], pre_grad), turned_ref[...])
    blocks_ref[0] = upper_blocks_ref[0] + send
    blocks_ref[1] = upper_blocks_ref[1] + recv
    blocks_ref[2] = kept_ref[...].astype(F32) + given_ref[...].astype(F32)
    if len(out_refs) == 1:
        out_refs[0][...] = blocks_ref[...].astype(BF16)
        return
    rows = D // len(out_refs)
    for step, ref in enumerate(out_refs):
        start = pl.multiple_of((lax.axis_index("patch") ^ step) * rows, rows)
        ref[...] = blocks_ref[:, pl.ds(start, rows), :].astype(BF16)


def first_backward_kernel(
    gather_ref, sum_ref, slope_ref, upper_grad_ref, upper_sums_ref, got_first_ref, got_second_ref, w_ref,
    grad_ref, sums_ref, first_ref, second_ref, pre_ref,
):
    send = upper_sums_ref[C_DEV : 2 * C_DEV, :] + rim_totals(got_first_ref, got_second_ref)
    grad = project(upper_grad_ref[...], send, upper_sums_ref[0:C_DEV, :], w_ref[0], w_ref[1])
    grad_ref[...] = grad
    layer_backward(gather_ref, sum_ref, slope_ref, grad, pre_ref, sums_ref)
    store_rim_sums(first_ref, second_ref, sums_ref)


def finish_kernel(grad_ref, sums_ref, got_first_ref, got_second_ref, w_ref, pool_ref, base_ref, out_ref):
    send = sums_ref[C_DEV : 2 * C_DEV, :] + rim_totals(got_first_ref, got_second_ref)
    grad = project(grad_ref[...], send, sums_ref[0:C_DEV, :], w_ref[0], w_ref[1])
    rows = base_ref.shape[0]
    hot = one_hot(iota((rows, C_DEV), 1) == columns_of(pool_ref[...] - node_base()))
    pulled = dot(jnp.concatenate([hot, hot], axis=1), stacked(0.125 * grad))
    out_ref[...] = (base_ref[...] + pulled).astype(BF16)


def exchange(x, axis, bit):
    return lax.ppermute(x, axis, [(i, i ^ bit) for i in range(lax.axis_size(axis))])


def bits_of(axis):
    return [1 << b for b in range(lax.axis_size(axis).bit_length() - 1)]


def group_sum(x):
    for bit in bits_of("sub"):
        x = x + exchange(x, "sub", bit)
    x = x.astype(BF16)
    *early, last = bits_of("rep")
    for bit in early:
        x = (x.astype(F32) + exchange(x, "rep", bit).astype(F32)).astype(BF16)
    return x, exchange(x, "rep", last)


def group_edges(x):
    for axis in ("sub", "rep"):
        for bit in bits_of(axis):
            x = jnp.concatenate([x, exchange(x, axis, bit)], axis=1)
    return x


def pair_trade(x, odd_pairs, flip):
    patches, reps = lax.axis_size("patch"), lax.axis_size("rep")
    moves = []
    for q in range(patches):
        for r in range(reps):
            partner = (q ^ 1) if not odd_pairs else (((q + 1) ^ 1) - 1)
            if 0 <= partner < patches:
                moves.append((q * reps + r, partner * reps + (r ^ flip)))
            else:
                moves.append((q * reps + r, q * reps + (r ^ 1)))
    return lax.ppermute(x, ("patch", "rep"), moves)


def trade(first, second, flip=0):
    return pair_trade(first, False, flip), pair_trade(second, True, flip)


def place_kernel(*refs):
    *blocks, out_ref = refs
    width = blocks[0].shape[2]
    for mask, ref in enumerate(blocks):
        start = pl.multiple_of((replica_index() ^ mask) * width, width)
        out_ref[:, :, pl.ds(start, width)] = ref[...].astype(F32)


def group_columns(x, beside):
    blocks = [x]
    for bit in bits_of("rep"):
        blocks = blocks + [exchange(block, "rep", bit) for block in blocks]
    blocks[-1], beside = lax.optimization_barrier((blocks[-1], beside))
    for bit in bits_of("sub"):
        blocks = blocks + [exchange(block, "sub", bit) for block in blocks]
    kinds, rows, width = x.shape
    if width % 128 == 0:
        return call(place_kernel, [((kinds, rows, D), F32)], *blocks)[0], beside
    order = jnp.arange(len(blocks)) ^ replica_index()
    ordered = jnp.take(jnp.stack(blocks), order, axis=0)
    return jnp.moveaxis(ordered, 0, 2).reshape(kinds, rows, D).astype(F32), beside


def per_device(
    fine_latents, out_cotangent, weights, pool_index, unpool_index, senders, receivers, edge_valid
):
    patches, reps, subs = (lax.axis_size(axis) for axis in ("patch", "rep", "sub"))
    rows = fine_latents.shape[0]
    slots = senders.shape[0]
    edges = slots * reps * subs
    width = D // (reps * subs)
    pool_row, unpool_row = pool_index[None, :], unpool_index[None, :]
    rim = ((RIM, D), BF16)
    coarse_out = ((C_DEV, D), F32)
    sums_out = ((SUMS, D), F32)
    work = [pltpu.VMEM((edges, D), BF16)]

    hot = (iota((C_DEV, rows), 0) == pool_row - node_base()).astype(BF16)
    pooled = dot(hot, fine_latents)
    own_edges = call(
        edges_kernel, [((2, slots), jnp.int32)], senders[None, :], receivers[None, :], edge_valid[None, :]
    )[0]
    part, first, second = call(pooled_kernel, [((C_DEV, D), BF16), rim, rim], pooled, exchange(pooled, "sub", 1))
    parts = [part] + [exchange(part, "rep", flip) for flip in range(1, reps)]
    got = [x for flip in range(reps) for x in trade(first, second, flip)]
    gather_hot, sum_hot = call(
        hots_kernel, [((edges, GATHER), BF16), ((SUMS, edges), BF16)], group_edges(own_edges), weights
    )
    near_out = ((edges, D), F32)
    slope_out = ((edges, D), BF16)
    rims_out = ((2 * RIM, D), BF16)
    coarse_0, near = call(first_near_kernel, [coarse_out, near_out], gather_hot, weights, *parts)
    got, near = lax.optimization_barrier((got, near))
    coarse_1, slope_1, rims_0, first, second = call(
        first_forward_kernel, [coarse_out, slope_out, rims_out, rim, rim],
        gather_hot, sum_hot, near, coarse_0, weights, *got, scratch=work,
    )
    got = trade(first, second)
    near, fine_half, hot_rows, hot_cols = call(
        near_kernel, [near_out, ((rows, D), F32), ((rows, 2 * C_DEV), BF16), ((C_DEV, rows), BF16)],
        gather_hot, weights, coarse_1, fine_latents, unpool_row,
    )
    got, near = lax.optimization_barrier((got, near))
    slope_2, rims_1, unpool_grad, partial = call(
        last_forward_kernel, [slope_out, rims_out, ((rows, D), BF16), coarse_out],
        gather_hot, sum_hot, near, coarse_1, weights, *got, fine_half, hot_rows, hot_cols, out_cotangent, scratch=work,
    )
    own, other = group_sum(partial)
    fine_base, kept, given = call(
        unpool_kernel, [((rows, D), F32), ((D, D // 2), BF16), ((D, D // 2), BF16)],
        fine_latents, out_cotangent, unpool_grad, weights,
    )
    given = exchange(given, "sub", 1)
    grad_2, sums_2, first, second = call(
        last_backward_kernel, [coarse_out, sums_out, rim, rim],
        gather_hot, sum_hot, slope_2, own, other, scratch=work,
    )
    for bit in reversed(bits_of("rep")):
        half = ((D, kept.shape[1] // 2), BF16)
        kept, given = call(functools.partial(halve_kernel, bit), [half, half], kept, given)
        given = exchange(given, "rep", bit)
    got = trade(first, second)
    blocks_2, turned, flowing = call(
        middle_kernel, [((2, D, width), F32), ((D, 2 * C_DEV + 4 * RIM), BF16), ((edges, width), F32)],
        gather_hot, grad_2, sums_2, weights, coarse_1, rims_1, coarse_0, rims_0,
    )
    got, flowing = lax.optimization_barrier((got, flowing))
    count = patches if patches <= 8 else 1
    blocks = call(
        block_backward_kernel, [((3, D // count, width), BF16)] * count,
        gather_hot, sum_hot, slope_1, flowing, *got, weights, turned, blocks_2, kept, given,
        scratch=[pltpu.VMEM((3, D, width), F32)],
    )
    if count == 1:
        moved = [lax.psum_scatter(blocks[0], "patch", scatter_dimension=1, tiled=True)]
    else:
        moved = [blocks[0]] + [exchange(blocks[step], "patch", step) for step in range(1, count)]
    grad_1, sums_1, first, second = call(
        first_backward_kernel, [coarse_out, sums_out, rim, rim],
        gather_hot, sum_hot, slope_1, grad_2, sums_2, *got, weights, scratch=work,
    )
    got = trade(first, second)
    moved, got = lax.optimization_barrier((moved, got))
    fine_grad = call(
        finish_kernel, [((rows, D), BF16)], grad_1, sums_1, *got, weights, pool_row, fine_base
    )[0]
    moved = sum(block.astype(F32) for block in moved).astype(BF16)
    weight_grads, fine_grad = group_columns(moved, fine_grad)
    return fine_grad, weight_grads


def solution(mesh):
    split = P(("patch", "rep", "sub"))
    rows = P(("member", "patch", "rep", "sub"), None)
    return jax.shard_map(
        per_device,
        mesh=mesh,
        in_specs=(rows, rows, P(), split, split, split, split, split),
        out_specs=(rows, P("member", "patch", None)),
        check_vma=False,
    )
```
